256 devices in a mesh: dp: 16 (over z_hi, x, core), mp: 16 (over y, z_lo).
Axes of the slice: x: 4, y: 4, z: 8 (z_hi: 2, z_lo: 4; z = z_hi * 4 + z_lo), core: 2. Of those that a mesh axis runs over, the one named last changes fastest.
Arguments:
- tokens: bfloat16 [2048, 4096], P('dp', 'mp'), may hold values from -6 to 6
- cotangent: bfloat16 [2048, 4096], P('dp', 'mp'), may hold values from -6 to 6
- gate_blocks: bfloat16 [128, 2048, 128], P('mp', 'dp'), may hold values from -0.125 to 0.125
- up_blocks: bfloat16 [128, 2048, 128], P('mp', 'dp'), may hold values from -0.125 to 0.125
- down_blocks: bfloat16 [128, 128, 2048], P('mp', None, 'dp'), may hold values from -0.0625 to 0.0625
- owner: int32 [112], replicated, may hold values from 0 to 15, as said below
- up_rows: int32 [112, 16], replicated, may hold values from 0 to 31, as said below
- down_cols: int32 [112, 16], replicated, may hold values from 0 to 31, as said below
Outputs:
- output: bfloat16 [2048, 4096], P('dp', 'mp')
- input_grad: bfloat16 [2048, 4096], P('dp', 'mp')
- gate_grad: float32 [128, 2048, 128], P('mp', 'dp')
- up_grad: float32 [128, 2048, 128], P('mp', 'dp')
- down_grad: float32 [128, 128, 2048], P('mp', None, 'dp')
The draws below stay inside these ranges and needn't reach their ends.
Inputs may be any that keep to these rules, and one draw needn't show every extreme that they name: Each owner holds at most 8 hidden blocks and some owner holds exactly 8. `up_rows`: each row lists 16 different row blocks. `down_cols`: each row lists 16 different column blocks.
All inputs are finite; a program needn't handle non-finite values.
Results may differ from the reference program's by a relative error of at most 0.022.
Values may be sent and summed in bfloat16 or wider, within the bound.
No kernel may reach another device: no remote copies, remote signals or barrier semaphores. Data moves between devices by JAX's collectives and lax.ppermute only.
A program may use at most 128 MiB of HBM per device.

```python
import jax
import jax.numpy as jnp
from jax import lax

D = 4096
FF = 14336
BLK = 128
TOK_DEV = 128
TOKENS = 2048
KD = 32
NZ = 16
KF = 112
CAP = 8
N_DP = 16
N_MP = 16


def draw_owner(key, part):
    key = jax.random.fold_in(key, 11)
    key_order, key_shift, key_shuffle = jax.random.split(key, 3)
    mean_load = KF // N_MP
    extra = CAP - mean_load
    halfway = N_MP // 2
    order = jax.random.permutation(key_order, N_MP)
    shifts = jax.random.randint(key_shift, (halfway,), 0, extra + 1).astype(jnp.int32)
    shifts = shifts.at[0].set(extra)
    loads = jnp.zeros((N_MP,), jnp.int32)
    loads = loads.at[order[:halfway]].add(mean_load + shifts)
    loads = loads.at[order[halfway:]].add(mean_load - shifts)
    limits = jnp.cumsum(loads)
    places = jnp.arange(KF, dtype=jnp.int32)
    sequence = jnp.sum((places[:, None] >= limits[None, :]).astype(jnp.int32), 1)
    shuffle = jax.random.permutation(key_shuffle, KF)
    return sequence[shuffle].astype(jnp.int32)


def block_lists(key):
    subkeys = jax.random.split(key, KF)
    orders = jax.vmap(lambda single: jax.random.permutation(single, KD))(subkeys)
    return orders[:, :NZ].astype(jnp.int32)


def draw_up_rows(key, part):
    key = jax.random.fold_in(key, 23)
    return block_lists(key)


def draw_down_cols(key, part):
    key = jax.random.fold_in(key, 37)
    return block_lists(key)


def shard_levels(own_key, extent, shards, least, top_value):
    loudness = 1.0
    for dim, blocks in shards:
        heights = jax.random.uniform(jax.random.fold_in(jax.random.fold_in(own_key, 6), dim), (blocks,), jnp.float32, least / len(shards), top_value / len(shards))
        loudness = loudness * jnp.repeat(jnp.exp(heights), extent[dim] // blocks).reshape((-1,) + (1,) * (len(extent) - 1 - dim))
    return loudness


def normal_values(rng, dims, spread, bound, shards=(), held_as=jnp.bfloat16):
    entries = spread * jax.random.normal(rng, dims, jnp.float32)
    if shards:
        entries = entries * shard_levels(rng, dims, shards, -0.22, 0.18)
    return jnp.clip(entries, -bound, bound).astype(held_as)


def setup_inputs(seed: int = 0) -> dict:
    seeds = jax.random.split(jax.random.key(seed), 9)
    return {
        "tokens": normal_values(seeds[0], (TOKENS, D), 1.0, 6.0, ((0, 16), (1, 16))),
        "cotangent": normal_values(seeds[1], (TOKENS, D), 1.0, 6.0, ((0, 16), (1, 16))),
        "gate_blocks": normal_values(seeds[2], (N_MP * CAP, NZ * BLK, BLK), (NZ * BLK) ** -0.5, 0.125, ((0, 16), (1, 16))),
        "up_blocks": normal_values(seeds[3], (N_MP * CAP, NZ * BLK, BLK), (NZ * BLK) ** -0.5, 0.125, ((0, 16), (1, 16))),
        "down_blocks": normal_values(seeds[4], (N_MP * CAP, BLK, NZ * BLK), (FF // 2) ** -0.5, 0.0625, ((0, 16), (2, 16))),
        "owner": draw_owner(jax.random.fold_in(seeds[8], 71), 0),
        "up_rows": draw_up_rows(jax.random.fold_in(seeds[8], 71), 0),
        "down_cols": draw_down_cols(jax.random.fold_in(seeds[8], 71), 0),
    }


def slot_tables(owner, up_rows, down_cols, owner_at, owner_count, capacity):
    onehot = (owner[:, None] == jnp.arange(owner_count, dtype=jnp.int32)[None, :]).astype(jnp.int32)
    ranks = jnp.sum(jnp.cumsum(onehot, 0) * onehot, 1) - 1
    select = ((owner[None, :] == owner_at) & (ranks[None, :] == jnp.arange(capacity, dtype=jnp.int32)[:, None])).astype(jnp.int32)
    row_ids = jnp.sum(select[:, :, None] * up_rows[None, :, :], 1).astype(jnp.int32)
    col_ids = jnp.sum(select[:, :, None] * down_cols[None, :, :], 1).astype(jnp.int32)
    live_mask = jnp.sum(select, 1).astype(jnp.float32)
    return row_ids, col_ids, live_mask


def pick_blocks(values, ids, block_size):
    count = values.shape[0]
    shaped = values.reshape(count, values.shape[1] // block_size, block_size)
    taken = jnp.take(shaped, ids.reshape(-1), axis=1)
    return taken.reshape(count, ids.shape[0], ids.shape[1] * block_size)


def place_blocks(terms, ids, live_mask, row_blocks, block_size):
    count = terms.shape[0]
    slots = ids.shape[0] * ids.shape[1]
    flags = (ids.reshape(-1)[:, None] == jnp.arange(row_blocks, dtype=jnp.int32)[None, :]).astype(jnp.float32)
    flags = flags * jnp.repeat(live_mask, ids.shape[1])[:, None]
    placed = jnp.einsum("tsb,sk->tkb", terms.reshape(count, slots, block_size), flags, precision=lax.Precision.HIGHEST)
    return placed.reshape(count, row_blocks * block_size)


def owner_pass(features, grad_out, gate_full, up_full, down_full, row_ids, col_ids, live_mask):
    f32 = jnp.float32
    block_size = gate_full.shape[2]
    row_blocks = features.shape[1] // block_size
    picked = pick_blocks(features, row_ids, block_size)
    gate_pre = jnp.einsum("tck,ckh->tch", picked.astype(f32), gate_full.astype(f32))
    up_pre = jnp.einsum("tck,ckh->tch", picked.astype(f32), up_full.astype(f32))
    sig_gate = jax.nn.sigmoid(gate_pre)
    hidden = (live_mask[None, :, None] * gate_pre * sig_gate * up_pre).astype(jnp.bfloat16)
    down_terms = jnp.einsum("tch,chk->tck", hidden.astype(f32), down_full.astype(f32))
    out_part = place_blocks(down_terms, col_ids, live_mask, row_blocks, block_size)
    picked_grad = pick_blocks(grad_out, col_ids, block_size)
    grad_hidden = live_mask[None, :, None] * jnp.einsum("tck,chk->tch", picked_grad.astype(f32), down_full.astype(f32))
    down_part = jnp.einsum("tch,tck->chk", hidden.astype(f32), picked_grad.astype(f32))
    up_term = (grad_hidden * gate_pre * sig_gate).astype(jnp.bfloat16)
    gate_term = (grad_hidden * up_pre * sig_gate * (1.0 + gate_pre * (1.0 - sig_gate))).astype(jnp.bfloat16)
    gate_part = jnp.einsum("tck,tch->ckh", picked.astype(f32), gate_term.astype(f32))
    up_part = jnp.einsum("tck,tch->ckh", picked.astype(f32), up_term.astype(f32))
    in_terms = jnp.einsum("tch,ckh->tck", gate_term.astype(f32), gate_full.astype(f32))
    in_terms = in_terms + jnp.einsum("tch,ckh->tck", up_term.astype(f32), up_full.astype(f32))
    in_part = place_blocks(in_terms, row_ids, live_mask, row_blocks, block_size)
    return out_part, in_part, gate_part, up_part, down_part


def rounded(values):
    return lax.optimization_barrier(values.astype(jnp.bfloat16)).astype(jnp.float32)


def reference(tokens, cotangent, gate_blocks, up_blocks, down_blocks, owner, up_rows, down_cols):
    f32 = jnp.float32

    def per_owner(sums, owner_at):
        row_ids, col_ids, live_mask = slot_tables(owner, up_rows, down_cols, owner_at, N_MP, CAP)
        start = (owner_at * CAP).astype(jnp.int32)
        gate_full = lax.dynamic_slice_in_dim(gate_blocks, start, CAP, 0)
        up_full = lax.dynamic_slice_in_dim(up_blocks, start, CAP, 0)
        down_full = lax.dynamic_slice_in_dim(down_blocks, start, CAP, 0)

        def per_shard(grads, shard):
            begin = (shard * TOK_DEV).astype(jnp.int32)
            features = lax.dynamic_slice_in_dim(tokens, begin, TOK_DEV, 0)
            grad_out = lax.dynamic_slice_in_dim(cotangent, begin, TOK_DEV, 0)
            out_part, in_part, gate_part, up_part, down_part = owner_pass(features, grad_out, gate_full, up_full, down_full, row_ids, col_ids, live_mask)
            grads = (grads[0] + rounded(gate_part), grads[1] + rounded(up_part), grads[2] + rounded(down_part))
            return grads, (out_part.astype(jnp.bfloat16), in_part.astype(jnp.bfloat16))

        zeros = (jnp.zeros(gate_full.shape, f32), jnp.zeros(up_full.shape, f32), jnp.zeros(down_full.shape, f32))
        grads, parts = lax.scan(per_shard, zeros, jnp.arange(N_DP, dtype=jnp.int32))
        out_all = parts[0].reshape(TOKENS, D).astype(f32)
        in_all = parts[1].reshape(TOKENS, D).astype(f32)
        return (sums[0] + out_all, sums[1] + in_all), grads

    start_sums = (jnp.zeros((TOKENS, D), f32), jnp.zeros((TOKENS, D), f32))
    sums, grads = lax.scan(per_owner, start_sums, jnp.arange(N_MP, dtype=jnp.int32))
    gate_grad = grads[0].reshape(N_MP * CAP, NZ * BLK, BLK)
    up_grad = grads[1].reshape(N_MP * CAP, NZ * BLK, BLK)
    down_grad = grads[2].reshape(N_MP * CAP, BLK, NZ * BLK)
    return sums[0].astype(jnp.bfloat16), sums[1].astype(jnp.bfloat16), gate_grad, up_grad, down_grad
```

```python
import functools

import jax
import jax.numpy as jnp
from jax import lax
from jax.experimental import pallas as pl
from jax.experimental.pallas import tpu as pltpu
from jax.sharding import Mesh, PartitionSpec as P

BF16 = jnp.bfloat16
F32 = jnp.float32
BLK = 128
HALF = 4
PIECES = 8
CHUNKS = 1


def rot(value, axis, step):
    n = lax.axis_size(axis)
    return lax.ppermute(value, axis, [(i, (i + step) % n) for i in range(n)])


def dot(a, b, ca, cb):
    return lax.dot_general(a, b, (((ca,), (cb,)), ((), ())), preferred_element_type=F32)


def layer_kernel(first, last, slots, *refs):
    up_ids, down_ids, live = refs[:3]
    acts = refs[3:11]
    at = 11
    carried = ()
    if not first:
        carried = refs[at : at + 2]
        at += 2
    weights = refs[at : at + PIECES]
    at += PIECES
    own_out, other_out = refs[at : at + 2]
    at += 2
    grads = refs[at : at + PIECES]
    at += PIECES
    xv, acc, pk, pg, wgu, wd, sems = refs[at:]
    s = pl.program_id(0)

    @pl.when(s == 0)
    def _():
        for i in range(8):
            pltpu.make_async_copy(
                acts[i], xv.at[i // 4, pl.ds((i % 4) * 8, 8)], sems.at[i]
            ).start()
        acc[...] = jnp.zeros_like(acc)
        for i in range(8):
            pltpu.make_async_copy(
                acts[i], xv.at[i // 4, pl.ds((i % 4) * 8, 8)], sems.at[i]
            ).wait()

    for b in range(16):
        u = up_ids[s, b]
        d = down_ids[s, b]
        cols = slice(b * BLK, (b + 1) * BLK)
        for c in range(2):
            rows = slice(c * BLK, (c + 1) * BLK)
            pk[rows, cols] = xv[c, u, 0]
            pg[rows, cols] = xv[c, d, 1]
        w = weights[b // 2]
        wgu[cols, 0:BLK] = w[b % 2, 0, 0]
        wgu[cols, BLK : 2 * BLK] = w[b % 2, 0, 1]
        wd[:, cols] = w[b % 2, 0, 2]

    alive = live[s]
    gate_up = dot(pk[...], wgu[...], 1, 0)
    gate = gate_up[:, :BLK]
    up = gate_up[:, BLK:]
    grad_hidden = alive * dot(pg[...], wd[...], 1, 1)
    sig = jax.nn.sigmoid(gate)
    hidden = (alive * gate * sig * up).astype(BF16)
    up_term = (grad_hidden * gate * sig).astype(BF16)
    gate_term = (grad_hidden * up * sig * (1.0 + gate * (1.0 - sig))).astype(BF16)
    terms = jnp.concatenate([gate_term, up_term], axis=1)

    for q in range(4):
        cols = slice(q * 512, (q + 1) * 512)
        out_terms = dot(hidden, wd[:, cols], 1, 0)
        in_terms = dot(terms, wgu[cols, :], 1, 1)
        dgu = dot(pk[:, cols], terms, 0, 0)
        dd = dot(hidden, pg[:, cols], 0, 0)
        for r in range(4):
            b = q * 4 + r
            part = slice(r * BLK, (r + 1) * BLK)
            u = up_ids[s, b]
            d = down_ids[s, b]
            acc[d, 0] += out_terms[:, part]
            acc[u, 1] += in_terms[:, part]
            g = grads[b // 2]
            g[b % 2, 0, 0] = dgu[part, :BLK].astype(BF16)
            g[b % 2, 0, 1] = dgu[part, BLK:].astype(BF16)
            g[b % 2, 0, 2] = dd[:, part].astype(BF16)

    @pl.when(s == slots - 1)
    def _():
        own = acc[:, :, :BLK, :]
        other = acc[:, :, BLK:, :]
        if not first:
            own = own + carried[0][...].astype(F32)
            other = other + carried[1][...].astype(F32)
        own_out[...] = own.astype(BF16)
        other_out[...] = other.astype(BF16)


def layer(first, last, up_ids, down_ids, live, acts, carried, weights):
    slots = weights[0].shape[1]
    smem = pl.BlockSpec(memory_space=pltpu.SMEM)
    anys = pl.BlockSpec(memory_space=pl.ANY)
    whole = pl.BlockSpec((32, 2, BLK, BLK), lambda s: (0, 0, 0, 0), pipeline_mode=pl.Buffered(1))
    piece = pl.BlockSpec((2, 1, 3, BLK, BLK), lambda s: (0, s, 0, 0, 0))
    part = jax.ShapeDtypeStruct((32, 2, BLK, BLK), BF16)
    grad = jax.ShapeDtypeStruct(weights[0].shape, BF16)
    outs = pl.pallas_call(
        functools.partial(layer_kernel, first, last, slots),
        grid=(slots,),
        in_specs=[smem] * 3 + [anys] * 8 + [whole] * len(carried) + [piece] * PIECES,
        out_specs=[whole] * 2 + [piece] * PIECES,
        out_shape=[part] * 2 + [grad] * PIECES,
        scratch_shapes=[
            pltpu.VMEM((2, 32, 2, BLK, BLK), BF16),
            pltpu.VMEM((32, 2, 2 * BLK, BLK), F32),
            pltpu.VMEM((2 * BLK, 2048), BF16),
            pltpu.VMEM((2 * BLK, 2048), BF16),
            pltpu.VMEM((2048, 2 * BLK), BF16),
            pltpu.VMEM((BLK, 2048), BF16),
            pltpu.SemaphoreType.DMA((8,)),
        ],
        compiler_params=pltpu.CompilerParams(vmem_limit_bytes=48 * 1024 * 1024),
        cost_estimate=pl.CostEstimate(
            flops=slots * 1_200_000_000, bytes_accessed=16 * 1024 * 1024, transcendentals=0
        ),
        name="layer",
    )(up_ids, down_ids, live, *acts, *carried, *weights)
    return outs[:2], outs[2:]


def tables(owner, up_rows, down_cols):
    zh, x, c = (lax.axis_index(a) for a in ("zh", "x", "c"))
    y, zl = lax.axis_index("y"), lax.axis_index("zl")
    me = y * 4 + zl
    count = owner.shape[0]
    f = jnp.arange(count, dtype=jnp.int32)
    earlier = (owner[None, :] == me) & (f[None, :] < f[:, None])
    rank = jnp.sum(earlier.astype(jnp.int32), 1)
    slot = c * HALF + jnp.arange(HALF, dtype=jnp.int32)
    select = ((owner == me)[None, :] & (rank[None, :] == slot[:, None])).astype(jnp.int32)
    b = jnp.arange(16, dtype=jnp.int32)
    held = (zh ^ ((b // 2) % 2)) * 8 + ((x - b // 4) % 4) * 2 + (c ^ (b % 2))

    def ids(table):
        raw = jnp.sum(select[:, :, None] * jnp.take(table, held, axis=1)[None], 1)
        home = raw // 2
        return (((y - home // 4) % 4) * 4 + (zl - home % 4) % 4) * 2 + raw % 2

    live = jnp.sum(select, 1).astype(F32)
    return ids(up_rows), ids(down_cols), live


def add(*values):
    return sum(v.astype(F32) for v in values)


def shards(tokens, cotangent, gate_blocks, up_blocks, down_blocks, owner, up_rows, down_cols):
    c = lax.axis_index("c")
    up_ids, down_ids, live = tables(owner, up_rows, down_cols)

    acts = jnp.stack([tokens, cotangent]).reshape(2, BLK, 2, BLK).transpose(2, 0, 1, 3)
    line = jnp.concatenate([acts] + [rot(acts, "zl", k) for k in (1, 2, 3)])
    ring = [line] + [rot(line, "y", k) for k in (1, 2, 3)]
    ring = ring + [rot(v, "c", 1) for v in ring]

    packed = jnp.stack([gate_blocks, up_blocks, down_blocks], 1)
    mine = lax.dynamic_slice_in_dim(packed, c * HALF, HALF, 0)
    theirs = lax.dynamic_slice_in_dim(packed, (1 - c) * HALF, HALF, 0)
    base = jnp.stack([mine, rot(theirs, "c", 1)])

    size = HALF // CHUNKS
    parts = ()
    sums = []
    for n in range(CHUNKS):
        take = slice(n * size, (n + 1) * size)
        near = base[:, take]
        far = rot(near, "zh", 1)
        weights = [near, far]
        for k in (1, 2, 3):
            weights += [rot(near, "x", k), rot(far, "x", k)]
        parts, grads = layer(
            n == 0, n == CHUNKS - 1, up_ids[take], down_ids[take], live[take], ring, parts, weights
        )
        far_sum = add(grads[1], *[rot(grads[2 * k + 1], "x", -k) for k in (1, 2, 3)]).astype(BF16)
        near_sum = add(grads[0], *[rot(grads[2 * k], "x", -k) for k in (1, 2, 3)])
        sums.append(add(near_sum, rot(far_sum, "zh", 1)))
    total = jnp.concatenate(sums, 1)
    received = rot(total[1].astype(BF16), "c", 1).astype(F32)
    lower = jnp.where(c == 0, total[0], received)
    upper = jnp.where(c == 0, received, total[0])
    grads = [jnp.concatenate([lower[:, i], upper[:, i]]) for i in range(3)]

    both = add(parts[0], rot(parts[1], "c", 1)).astype(BF16)
    both = both.reshape(4, 8, 2, BLK, BLK)
    line = add(both[0], *[rot(both[k], "y", -k) for k in (1, 2, 3)]).astype(BF16)
    line = line.reshape(4, 2, 2, BLK, BLK)
    done = add(line[0], *[rot(line[k], "zl", -k) for k in (1, 2, 3)]).astype(BF16)
    done = done.transpose(1, 2, 0, 3).reshape(2, BLK, 2 * BLK)
    return (done[0], done[1], *grads)


def solution(mesh):
    fine = Mesh(mesh.devices.reshape(2, 4, 2, 4, 4), ("zh", "x", "c", "y", "zl"))
    dp = ("zh", "x", "c")
    mp = ("y", "zl")
    return jax.shard_map(
        shards,
        mesh=fine,
        in_specs=(P(dp, mp), P(dp, mp), P(mp, dp, None), P(mp, dp, None), P(mp, None, dp), P(), P(), P()),
        out_specs=(P(dp, mp), P(dp, mp), P(mp, dp, None), P(mp, dp, None), P(mp, None, dp)),
        check_vma=False,
    )
```

```python
import functools

import jax
import jax.numpy as jnp
from jax import lax
from jax.experimental import pallas as pl
from jax.experimental.pallas import tpu as pltpu
from jax.sharding import Mesh, PartitionSpec as P

BF16 = jnp.bfloat16
F32 = jnp.float32
BLK = 128
HALF = 4
PLACES = [(0, 0), (0, 1), (1, 0), (1, 1), (2, 0), (2, 1), (3, 0), (4, 0)] + [(5 + p, j) for p in range(4) for j in (0, 1)]
PIECES = 9
CHUNKS = 2
LONG = 100_000_000_000


def rot(value, axis, step):
    n = lax.axis_size(axis)
    with jax.named_scope("Move_" + axis + str(step % n)):
        return lax.ppermute(value, axis, [(i, (i + step) % n) for i in range(n)])


def dot(a, b, ca, cb):
    return lax.dot_general(a, b, (((ca,), (cb,)), ((), ())), preferred_element_type=F32)


def layer_kernel(first, slots, *refs):
    up_ids, down_ids, live = refs[:3]
    acts = refs[3:5]
    at = 5
    carried = ()
    if not first:
        carried = refs[at : at + 2]
        at += 2 + 5
    weights = refs[at : at + PIECES]
    at += PIECES
    own_out, other_out = refs[at : at + 2]
    at += 2
    grads = refs[at : at + PIECES]
    at += PIECES
    xv, acc, pk, pg, wgu, wd, sems = refs[at:]
    s = pl.program_id(0)

    @pl.when(s == 0)
    def _():
        for i in range(2):
            pltpu.make_async_copy(acts[i], xv.at[i], sems.at[i]).start()
        acc[...] = jnp.zeros_like(acc)
        for i in range(2):
            pltpu.make_async_copy(acts[i], xv.at[i], sems.at[i]).wait()

    for b in range(16):
        u = up_ids[s, b]
        d = down_ids[s, b]
        cols = slice(b * BLK, (b + 1) * BLK)
        for c in range(2):
            rows = slice(c * BLK, (c + 1) * BLK)
            pk[rows, cols] = xv[c, u, 0]
            pg[rows, cols] = xv[c, d, 1]
        p, j = PLACES[b]
        wgu[cols, 0:BLK] = weights[p][j, 0, 0]
        wgu[cols, BLK : 2 * BLK] = weights[p][j, 0, 1]
        wd[:, cols] = weights[p][j, 0, 2]

    alive = live[s]
    gate_up = dot(pk[...], wgu[...], 1, 0)
    gate = gate_up[:, :BLK]
    up = gate_up[:, BLK:]
    grad_hidden = alive * dot(pg[...], wd[...], 1, 1)
    sig = jax.nn.sigmoid(gate)
    hidden = (alive * gate * sig * up).astype(BF16)
    up_term = (grad_hidden * gate * sig).astype(BF16)
    gate_term = (grad_hidden * up * sig * (1.0 + gate * (1.0 - sig))).astype(BF16)
    terms = jnp.concatenate([gate_term, up_term], axis=1)

    for q in range(4):
        cols = slice(q * 512, (q + 1) * 512)
        out_terms = dot(hidden, wd[:, cols], 1, 0)
        in_terms = dot(terms, wgu[cols, :], 1, 1)
        dgu = dot(pk[:, cols], terms, 0, 0)
        dd = dot(hidden, pg[:, cols], 0, 0)
        for r in range(4):
            b = q * 4 + r
            part = slice(r * BLK, (r + 1) * BLK)
            u = up_ids[s, b]
            d = down_ids[s, b]
            acc[d, 0] += out_terms[:, part]
            acc[u, 1] += in_terms[:, part]
            p, j = PLACES[b]
            grads[p][j, 0, 0] = dgu[part, :BLK].astype(BF16)
            grads[p][j, 0, 1] = dgu[part, BLK:].astype(BF16)
            grads[p][j, 0, 2] = dd[:, part].astype(BF16)

    @pl.when(s == slots - 1)
    def _():
        own = acc[:, :, :BLK, :]
        other = acc[:, :, BLK:, :]
        if not first:
            own = own + carried[0][...].astype(F32)
            other = other + carried[1][...].astype(F32)
        own_out[...] = own.astype(BF16)
        other_out[...] = other.astype(BF16)


def layer(start, up_ids, down_ids, live, acts, carried, weights):
    slots = HALF // CHUNKS
    first = not carried
    smem = pl.BlockSpec(memory_space=pltpu.SMEM)
    anys = pl.BlockSpec(memory_space=pl.ANY)
    whole = pl.BlockSpec((32, 2, BLK, BLK), lambda s: (0, 0, 0, 0), pipeline_mode=pl.Buffered(1))
    near = [pl.BlockSpec((w.shape[0], 1, 3, BLK, BLK), lambda s: (0, start + s, 0, 0, 0)) for w in weights[:5]]
    far = [pl.BlockSpec((w.shape[0], 1, 3, BLK, BLK), lambda s: (0, s, 0, 0, 0)) for w in weights[5:]]
    part = jax.ShapeDtypeStruct((32, 2, BLK, BLK), BF16)
    outs = pl.pallas_call(
        functools.partial(layer_kernel, first, slots),
        grid=(slots,),
        in_specs=[smem] * 3 + [anys] * 2 + [whole] * len(carried[:2]) + [anys] * len(carried[2:]) + near + far,
        out_specs=[whole] * 2 + near + far,
        out_shape=[part] * 2 + [jax.ShapeDtypeStruct(w.shape, BF16) for w in weights],
        input_output_aliases={} if first else {7 + i: 2 + i for i in range(5)},
        scratch_shapes=[
            pltpu.VMEM((2, 32, 2, BLK, BLK), BF16),
            pltpu.VMEM((32, 2, 2 * BLK, BLK), F32),
            pltpu.VMEM((2 * BLK, 2048), BF16),
            pltpu.VMEM((2 * BLK, 2048), BF16),
            pltpu.VMEM((2048, 2 * BLK), BF16),
            pltpu.VMEM((BLK, 2048), BF16),
            pltpu.SemaphoreType.DMA((2,)),
        ],
        compiler_params=pltpu.CompilerParams(vmem_limit_bytes=60 * 1024 * 1024),
        cost_estimate=pl.CostEstimate(
            flops=LONG, bytes_accessed=16 * 1024 * 1024, transcendentals=0
        ),
        name="layer",
    )(up_ids, down_ids, live, *acts, *carried, *weights)
    return outs[:2], outs[2:7], outs[7:]


def tables(owner, up_rows, down_cols):
    zh, x, c = (lax.axis_index(a) for a in ("zh", "x", "c"))
    zl = lax.axis_index("zl")
    me = lax.axis_index("y") * 4 + zl
    count = owner.shape[0]
    f = jnp.arange(count, dtype=jnp.int32)
    earlier = (owner[None, :] == me) & (f[None, :] < f[:, None])
    rank = jnp.sum(earlier.astype(jnp.int32), 1)
    slot = c * HALF + jnp.arange(HALF, dtype=jnp.int32)
    select = ((owner == me)[None, :] & (rank[None, :] == slot[:, None])).astype(jnp.int32)
    away = jnp.array([0, 0, 1, 1, 3, 3, 2, 2] * 2, jnp.int32)
    b = jnp.arange(16, dtype=jnp.int32)
    held = (zh ^ (b // 8)) * 8 + ((x - away) % 4) * 2 + (c ^ (b % 2))

    def ids(table):
        raw = jnp.sum(select[:, :, None] * jnp.take(table, held, axis=1)[None], 1)
        home = raw // 2
        return ((home // 4) * 4 + (zl - home % 4) % 4) * 2 + raw % 2

    live = jnp.sum(select, 1).astype(F32)
    return ids(up_rows), ids(down_cols), live


def add(*values):
    return sum(v.astype(F32) for v in values)


tie = lax.optimization_barrier


def neighbours(value):
    return rot(value, "x", 1), rot(value, "x", -1)


def opposite(left, right):
    return rot(left[:1], "x", 1), rot(right[1:], "x", -1)


def to_opposite(parts):
    return rot(parts[3], "x", -1), rot(parts[4], "x", 1)


def to_neighbours(parts, from_right, from_left):
    left = jnp.concatenate([add(parts[1][:1], from_right).astype(BF16), parts[1][1:]])
    right = jnp.concatenate([parts[2][:1], add(parts[2][1:], from_left).astype(BF16)])
    return add(parts[0], rot(left, "x", -1), rot(right, "x", 1))


def shards(tokens, cotangent, gate_blocks, up_blocks, down_blocks, owner, up_rows, down_cols):
    c = lax.axis_index("c")
    up_ids, down_ids, live = tables(owner, up_rows, down_cols)

    blocks = (gate_blocks, up_blocks, down_blocks)
    mine = jnp.stack([lax.dynamic_slice_in_dim(v, c * HALF, HALF, 0) for v in blocks], 1)
    theirs = jnp.stack([lax.dynamic_slice_in_dim(v, (1 - c) * HALF, HALF, 0) for v in blocks], 1)
    base = jnp.stack([mine, rot(theirs, "c", 1)])

    acts = jnp.stack([tokens, cotangent]).reshape(2, BLK, 2, BLK).transpose(2, 0, 1, 3)
    base, acts, up_ids, down_ids, live = tie((base, acts, up_ids, down_ids, live))
    lines = [acts] + [rot(acts, "zl", k) for k in (1, 2, 3)]
    near = neighbours(base)
    line, base = tie((jnp.concatenate(lines), base))
    ring = lax.all_gather(line, "y", axis=0, tiled=True)

    size = HALF // CHUNKS
    takes = [slice(n * size, (n + 1) * size) for n in range(CHUNKS)]
    first, second = [rot(base[:, take], "zh", 1) for take in takes]
    near = [base, *near, *opposite(*near)]
    first, near = tie((first, near))
    first = [first, *[rot(first, "x", k) for k in (1, 3)]]
    second, first = tie((second, first))
    first += [rot(first[0], "x", 2)]
    second, ring = tie((second, ring))
    second = [second, *[rot(second, "x", k) for k in (1, 3, 2)]]
    ring = [ring, rot(ring, "c", 1)]

    take = takes[0]
    parts, near_parts, far_parts = layer(0, up_ids[take], down_ids[take], live[take], ring, (), near + first)
    first_sum = add(far_parts[0], *[rot(far_parts[p], "x", k) for p, k in ((1, 3), (2, 1), (3, 2))]).astype(BF16)
    take = takes[1]
    parts, near_parts, far_parts = layer(
        size, up_ids[take], down_ids[take], live[take], ring, (*parts, *near_parts), near + second
    )
    parts, far_parts, near_parts, first_sum = tie((parts, far_parts, near_parts, first_sum))
    both = add(parts[0], rot(parts[1], "c", 1)).astype(BF16)
    first_sum = rot(first_sum, "zh", 1)
    second_sum = [far_parts[0], *[rot(far_parts[p], "x", k) for p, k in ((1, 3), (2, 1), (3, 2))]]
    both, second_sum = tie((both, second_sum))
    line = lax.psum_scatter(both, "y", scatter_dimension=0, tiled=True)
    some, near_parts, first_sum = tie((second_sum[:3], near_parts, first_sum))
    crossed = to_opposite(near_parts)
    second_sum = rot(add(*some, second_sum[3]).astype(BF16), "zh", 1)
    near_sum = to_neighbours(near_parts, *crossed)
    line, first_sum = tie((line, first_sum))
    line = line.reshape(4, 2, 2, BLK, BLK)
    lines = [line[0], *[rot(line[k], "zl", -k) for k in (1, 2, 3)]]
    near_sum, lines, second_sum = tie((near_sum, lines, second_sum))
    done = add(*lines).astype(BF16)
    done = done.transpose(1, 2, 0, 3).reshape(2, BLK, 2 * BLK)
    far_sums = [first_sum, second_sum]

    total = add(near_sum, jnp.concatenate(far_sums, 1))
    received = rot(total[1].astype(BF16), "c", 1).astype(F32)
    lower = jnp.where(c == 0, total[0], received)
    upper = jnp.where(c == 0, received, total[0])
    grads = [jnp.concatenate([lower[:, i], upper[:, i]]) for i in range(3)]
    return (done[0], done[1], *grads)


def solution(mesh):
    fine = Mesh(mesh.devices.reshape(2, 4, 2, 4, 4), ("zh", "x", "c", "y", "zl"))
    dp = ("zh", "x", "c")
    mp = ("y", "zl")
    return jax.shard_map(
        shards,
        mesh=fine,
        in_specs=(P(dp, mp), P(dp, mp), P(mp, dp, None), P(mp, dp, None), P(mp, None, dp), P(), P(), P()),
        out_specs=(P(dp, mp), P(dp, mp), P(mp, dp, None), P(mp, dp, None), P(mp, None, dp)),
        check_vma=False,
    )
```

```python
import functools

import jax
import jax.numpy as jnp
from jax import lax
from jax.experimental import pallas as pl
from jax.experimental.pallas import tpu as pltpu
from jax.sharding import Mesh, PartitionSpec as P

BF16 = jnp.bfloat16
F32 = jnp.float32
BLK = 128
HALF = 4
PLACES = [(0, 0), (0, 1), (1, 0), (1, 1), (2, 0), (2, 1), (3, 0), (4, 0)] + [(5 + p, j) for p in range(4) for j in (0, 1)]
PIECES = 9
CHUNKS = 2
SHORT = 17_000_000_000
LONG = 100_000_000_000


def rot(value, axis, step):
    n = lax.axis_size(axis)
    with jax.named_scope("Move_" + axis + str(step % n)):
        return lax.ppermute(value, axis, [(i, (i + step) % n) for i in range(n)])


def dot(a, b, ca, cb):
    return lax.dot_general(a, b, (((ca,), (cb,)), ((), ())), preferred_element_type=F32)


def layer_kernel(first, slots, *refs):
    up_ids, down_ids, live = refs[:3]
    acts = refs[3:5]
    at = 5
    carried = ()
    if not first:
        carried = refs[at : at + 2]
        at += 2 + 5
    weights = refs[at : at + PIECES]
    at += PIECES
    own_out, other_out = refs[at : at + 2]
    at += 2
    grads = refs[at : at + PIECES]
    at += PIECES
    xv, acc, pk, pg, wgu, wd, sems = refs[at:]
    s = pl.program_id(0)

    @pl.when(s == 0)
    def _():
        for i in range(2):
            pltpu.make_async_copy(acts[i], xv.at[i], sems.at[i]).start()
        acc[...] = jnp.zeros_like(acc)
        for i in range(2):
            pltpu.make_async_copy(acts[i], xv.at[i], sems.at[i]).wait()

    for b in range(16):
        u = up_ids[s, b]
        d = down_ids[s, b]
        cols = slice(b * BLK, (b + 1) * BLK)
        for c in range(2):
            rows = slice(c * BLK, (c + 1) * BLK)
            pk[rows, cols] = xv[c, u, 0]
            pg[rows, cols] = xv[c, d, 1]
        p, j = PLACES[b]
        wgu[cols, 0:BLK] = weights[p][j, 0, 0]
        wgu[cols, BLK : 2 * BLK] = weights[p][j, 0, 1]
        wd[:, cols] = weights[p][j, 0, 2]

    alive = live[s]
    gate_up = dot(pk[...], wgu[...], 1, 0)
    gate = gate_up[:, :BLK]
    up = gate_up[:, BLK:]
    grad_hidden = alive * dot(pg[...], wd[...], 1, 1)
    sig = jax.nn.sigmoid(gate)
    hidden = (alive * gate * sig * up).astype(BF16)
    up_term = (grad_hidden * gate * sig).astype(BF16)
    gate_term = (grad_hidden * up * sig * (1.0 + gate * (1.0 - sig))).astype(BF16)
    terms = jnp.concatenate([gate_term, up_term], axis=1)

    for q in range(4):
        cols = slice(q * 512, (q + 1) * 512)
        out_terms = dot(hidden, wd[:, cols], 1, 0)
        in_terms = dot(terms, wgu[cols, :], 1, 1)
        dgu = dot(pk[:, cols], terms, 0, 0)
        dd = dot(hidden, pg[:, cols], 0, 0)
        for r in range(4):
            b = q * 4 + r
            part = slice(r * BLK, (r + 1) * BLK)
            u = up_ids[s, b]
            d = down_ids[s, b]
            acc[d, 0] += out_terms[:, part]
            acc[u, 1] += in_terms[:, part]
            p, j = PLACES[b]
            grads[p][j, 0, 0] = dgu[part, :BLK].astype(BF16)
            grads[p][j, 0, 1] = dgu[part, BLK:].astype(BF16)
            grads[p][j, 0, 2] = dd[:, part].astype(BF16)

    @pl.when(s == slots - 1)
    def _():
        own = acc[:, :, :BLK, :]
        other = acc[:, :, BLK:, :]
        if not first:
            own = own + carried[0][...].astype(F32)
            other = other + carried[1][...].astype(F32)
        own_out[...] = own.astype(BF16)
        other_out[...] = other.astype(BF16)


def layer(start, up_ids, down_ids, live, acts, carried, weights):
    slots = HALF // CHUNKS
    first = not carried
    smem = pl.BlockSpec(memory_space=pltpu.SMEM)
    anys = pl.BlockSpec(memory_space=pl.ANY)
    whole = pl.BlockSpec((32, 2, BLK, BLK), lambda s: (0, 0, 0, 0), pipeline_mode=pl.Buffered(1))
    near = [pl.BlockSpec((w.shape[0], 1, 3, BLK, BLK), lambda s: (0, start + s, 0, 0, 0)) for w in weights[:5]]
    far = [pl.BlockSpec((w.shape[0], 1, 3, BLK, BLK), lambda s: (0, s, 0, 0, 0)) for w in weights[5:]]
    part = jax.ShapeDtypeStruct((32, 2, BLK, BLK), BF16)
    outs = pl.pallas_call(
        functools.partial(layer_kernel, first, slots),
        grid=(slots,),
        in_specs=[smem] * 3 + [anys] * 2 + [whole] * len(carried[:2]) + [anys] * len(carried[2:]) + near + far,
        out_specs=[whole] * 2 + near + far,
        out_shape=[part] * 2 + [jax.ShapeDtypeStruct(w.shape, BF16) for w in weights],
        input_output_aliases={} if first else {7 + i: 2 + i for i in range(5)},
        scratch_shapes=[
            pltpu.VMEM((2, 32, 2, BLK, BLK), BF16),
            pltpu.VMEM((32, 2, 2 * BLK, BLK), F32),
            pltpu.VMEM((2 * BLK, 2048), BF16),
            pltpu.VMEM((2 * BLK, 2048), BF16),
            pltpu.VMEM((2048, 2 * BLK), BF16),
            pltpu.VMEM((BLK, 2048), BF16),
            pltpu.SemaphoreType.DMA((2,)),
        ],
        compiler_params=pltpu.CompilerParams(vmem_limit_bytes=60 * 1024 * 1024),
        cost_estimate=pl.CostEstimate(
            flops=LONG, bytes_accessed=16 * 1024 * 1024, transcendentals=0
        ),
        name="layer",
    )(up_ids, down_ids, live, *acts, *carried, *weights)
    return outs[:2], outs[2:7], outs[7:]


def tables(owner, up_rows, down_cols):
    zh, x, c = (lax.axis_index(a) for a in ("zh", "x", "c"))
    zl = lax.axis_index("zl")
    me = lax.axis_index("y") * 4 + zl
    count = owner.shape[0]
    f = jnp.arange(count, dtype=jnp.int32)
    earlier = (owner[None, :] == me) & (f[None, :] < f[:, None])
    rank = jnp.sum(earlier.astype(jnp.int32), 1)
    slot = c * HALF + jnp.arange(HALF, dtype=jnp.int32)
    select = ((owner == me)[None, :] & (rank[None, :] == slot[:, None])).astype(jnp.int32)
    away = jnp.array([0, 0, 1, 1, 3, 3, 2, 2] * 2, jnp.int32)
    b = jnp.arange(16, dtype=jnp.int32)
    held = (zh ^ (b // 8)) * 8 + ((x - away) % 4) * 2 + (c ^ (b % 2))

    def ids(table):
        raw = jnp.sum(select[:, :, None] * jnp.take(table, held, axis=1)[None], 1)
        home = raw // 2
        return ((home // 4) * 4 + (zl - home % 4) % 4) * 2 + raw % 2

    live = jnp.sum(select, 1).astype(F32)
    return ids(up_rows), ids(down_cols), live


def add(*values):
    return sum(v.astype(F32) for v in values)


tie = lax.optimization_barrier


def neighbours(value):
    return rot(value, "x", 1), rot(value, "x", -1)


def copy_kernel(*refs):
    for source, target in zip(refs[: len(refs) // 2], refs[len(refs) // 2 :]):
        target[...] = source[...]


def add_kernel(left, right, from_right, from_left, new_left, new_right):
    new_left[0] = (left[0].astype(F32) + from_right[0].astype(F32)).astype(BF16)
    new_left[1] = left[1]
    new_right[0] = right[0]
    new_right[1] = (right[1].astype(F32) + from_left[0].astype(F32)).astype(BF16)


def small(kernel, values, shapes, earlier=()):
    whole = [pl.BlockSpec(memory_space=pltpu.VMEM)] * len(shapes)
    count = len(values)

    def body(*refs):
        kernel(*refs[:count], *refs[count + len(earlier) :])

    return pl.pallas_call(
        body,
        in_specs=[pl.BlockSpec(memory_space=pltpu.VMEM)] * count + [pl.BlockSpec(memory_space=pl.ANY)] * len(earlier),
        out_specs=whole,
        out_shape=[jax.ShapeDtypeStruct(v, BF16) for v in shapes],
        compiler_params=pltpu.CompilerParams(vmem_limit_bytes=32 * 1024 * 1024),
        cost_estimate=pl.CostEstimate(flops=SHORT, bytes_accessed=2 * 1024 * 1024, transcendentals=0),
        name=kernel.__name__,
    )(*values, *earlier)


def halves_kernel(left, right, first, second):
    first[...] = left[0:1]
    second[...] = right[1:2]


def shards(tokens, cotangent, gate_blocks, up_blocks, down_blocks, owner, up_rows, down_cols):
    c = lax.axis_index("c")
    up_ids, down_ids, live = tables(owner, up_rows, down_cols)

    blocks = (gate_blocks, up_blocks, down_blocks)
    mine = jnp.stack([lax.dynamic_slice_in_dim(v, c * HALF, HALF, 0) for v in blocks], 1)
    theirs = jnp.stack([lax.dynamic_slice_in_dim(v, (1 - c) * HALF, HALF, 0) for v in blocks], 1)
    base = jnp.stack([mine, rot(theirs, "c", 1)])

    acts = jnp.stack([tokens, cotangent]).reshape(2, BLK, 2, BLK).transpose(2, 0, 1, 3)
    base, acts, up_ids, down_ids, live = tie((base, acts, up_ids, down_ids, live))
    lines = [small(copy_kernel, (acts,), [acts.shape])[0]] + [rot(acts, "zl", k) for k in (1, 2, 3)]
    near = neighbours(base)
    line, base = tie((jnp.concatenate(lines), base))
    ring = lax.all_gather(line, "y", axis=0, tiled=True)

    size = HALF // CHUNKS
    takes = [slice(n * size, (n + 1) * size) for n in range(CHUNKS)]
    first, second = [rot(base[:, take], "zh", 1) for take in takes]
    cut = small(halves_kernel, near, [(1, *base.shape[1:])] * 2)
    near = [base, *near, rot(cut[0], "x", 1), rot(cut[1], "x", -1)]
    first, near = tie((first, near))
    first = [first, *[rot(first, "x", k) for k in (1, 3, 2)]]
    second, first, ring = tie((second, first, ring))
    second = [second, *[rot(second, "x", k) for k in (1, 3, 2)]]
    ring = [ring, rot(ring, "c", 1)]

    take = takes[0]
    parts, near_parts, far_parts = layer(0, up_ids[take], down_ids[take], live[take], ring, (), near + first)
    first_sum = add(far_parts[0], *[rot(far_parts[p], "x", k) for p, k in ((1, 3), (2, 1), (3, 2))]).astype(BF16)
    take = takes[1]
    parts, near_parts, far_parts = layer(
        size, up_ids[take], down_ids[take], live[take], ring, (*parts, *near_parts), near + second
    )
    parts, far_parts, near_parts, first_sum = tie((parts, far_parts, near_parts, first_sum))
    both = add(parts[0], rot(parts[1], "c", 1)).astype(BF16)
    first_sum = rot(first_sum, "zh", 1)
    second_sum = [far_parts[0], *[rot(far_parts[p], "x", k) for p, k in ((1, 3), (2, 1), (3, 2))]]
    line = lax.psum_scatter(both, "y", scatter_dimension=0, tiled=True)
    sent = small(copy_kernel, near_parts[3:], [v.shape for v in near_parts[3:]], [both])
    second_sum, sent, first_sum = tie((second_sum, sent, first_sum))
    second_sum = add(*second_sum).astype(BF16)
    crossed = rot(sent[0], "x", -1), rot(sent[1], "x", 1)
    left, right = small(add_kernel, (*near_parts[1:3], *crossed), [near_parts[1].shape] * 2, [second_sum])
    second_sum = rot(second_sum, "zh", 1)
    near_sum = add(near_parts[0], rot(left, "x", -1), rot(right, "x", 1))
    line = line.reshape(4, 2, 2, BLK, BLK)
    lines = [line[0], *[rot(line[k], "zl", -k) for k in (1, 2, 3)]]
    near_sum, lines, second_sum = tie((near_sum, lines, second_sum))
    done = add(*lines).astype(BF16)
    done = done.transpose(1, 2, 0, 3).reshape(2, BLK, 2 * BLK)
    far_sums = [first_sum, second_sum]

    total = add(near_sum, jnp.concatenate(far_sums, 1))
    received = rot(total[1].astype(BF16), "c", 1).astype(F32)
    lower = jnp.where(c == 0, total[0], received)
    upper = jnp.where(c == 0, received, total[0])
    grads = [jnp.concatenate([lower[:, i], upper[:, i]]) for i in range(3)]
    return (done[0], done[1], *grads)


def solution(mesh):
    fine = Mesh(mesh.devices.reshape(2, 4, 2, 4, 4), ("zh", "x", "c", "y", "zl"))
    dp = ("zh", "x", "c")
    mp = ("y", "zl")
    return jax.shard_map(
        shards,
        mesh=fine,
        in_specs=(P(dp, mp), P(dp, mp), P(mp, dp, None), P(mp, dp, None), P(mp, None, dp), P(), P(), P()),
        out_specs=(P(dp, mp), P(dp, mp), P(mp, dp, None), P(mp, dp, None), P(mp, None, dp)),
        check_vma=False,
    )
```

```python
import functools

import jax
import jax.numpy as jnp
from jax import lax
from jax.experimental import pallas as pl
from jax.experimental.pallas import tpu as pltpu
from jax.sharding import Mesh, PartitionSpec as P

BF16 = jnp.bfloat16
F32 = jnp.float32
BLK = 128
HALF = 4
PLACES = [(0, 0), (0, 1), (1, 0), (1, 1), (2, 0), (2, 1), (3, 0), (4, 0)] + [(5 + p, j) for p in range(4) for j in (0, 1)]
PIECES = 9
CHUNKS = 2
SHORT = 17_000_000_000
LONG = 100_000_000_000


def rot(value, axis, step):
    n = lax.axis_size(axis)
    with jax.named_scope("Move_" + axis + str(step % n)):
        return lax.ppermute(value, axis, [(i, (i + step) % n) for i in range(n)])


def dot(a, b, ca, cb):
    return lax.dot_general(a, b, (((ca,), (cb,)), ((), ())), preferred_element_type=F32)


def layer_kernel(first, slots, *refs):
    up_ids, down_ids, live = refs[:3]
    acts = refs[3:5]
    at = 5
    carried = ()
    if not first:
        carried = refs[at : at + 2]
        at += 2 + 5
    weights = refs[at : at + PIECES]
    at += PIECES
    own_out, other_out = refs[at : at + 2]
    at += 2
    grads = refs[at : at + PIECES]
    at += PIECES
    xv, acc, pk, pg, wgu, wd, sems = refs[at:]
    s = pl.program_id(0)

    @pl.when(s == 0)
    def _():
        for i in range(2):
            pltpu.make_async_copy(acts[i], xv.at[i], sems.at[i]).start()
        acc[...] = jnp.zeros_like(acc)
        for i in range(2):
            pltpu.make_async_copy(acts[i], xv.at[i], sems.at[i]).wait()

    for b in range(16):
        u = up_ids[s, b]
        d = down_ids[s, b]
        cols = slice(b * BLK, (b + 1) * BLK)
        for c in range(2):
            rows = slice(c * BLK, (c + 1) * BLK)
            pk[rows, cols] = xv[c, u, 0]
            pg[rows, cols] = xv[c, d, 1]
        p, j = PLACES[b]
        wgu[cols, 0:BLK] = weights[p][j, 0, 0]
        wgu[cols, BLK : 2 * BLK] = weights[p][j, 0, 1]
        wd[:, cols] = weights[p][j, 0, 2]

    alive = live[s]
    gate_up = dot(pk[...], wgu[...], 1, 0)
    gate = gate_up[:, :BLK]
    up = gate_up[:, BLK:]
    grad_hidden = alive * dot(pg[...], wd[...], 1, 1)
    sig = jax.nn.sigmoid(gate)
    hidden = (alive * gate * sig * up).astype(BF16)
    up_term = (grad_hidden * gate * sig).astype(BF16)
    gate_term = (grad_hidden * up * sig * (1.0 + gate * (1.0 - sig))).astype(BF16)
    terms = jnp.concatenate([gate_term, up_term], axis=1)

    for q in range(4):
        cols = slice(q * 512, (q + 1) * 512)
        out_terms = dot(hidden, wd[:, cols], 1, 0)
        in_terms = dot(terms, wgu[cols, :], 1, 1)
        dgu = dot(pk[:, cols], terms, 0, 0)
        dd = dot(hidden, pg[:, cols], 0, 0)
        for r in range(4):
            b = q * 4 + r
            part = slice(r * BLK, (r + 1) * BLK)
            u = up_ids[s, b]
            d = down_ids[s, b]
            acc[d, 0] += out_terms[:, part]
            acc[u, 1] += in_terms[:, part]
            p, j = PLACES[b]
            grads[p][j, 0, 0] = dgu[part, :BLK].astype(BF16)
            grads[p][j, 0, 1] = dgu[part, BLK:].astype(BF16)
            grads[p][j, 0, 2] = dd[:, part].astype(BF16)

    @pl.when(s == slots - 1)
    def _():
        own = acc[:, :, :BLK, :]
        other = acc[:, :, BLK:, :]
        if not first:
            own = own + carried[0][...].astype(F32)
            other = other + carried[1][...].astype(F32)
        own_out[...] = own.astype(BF16)
        other_out[...] = other.astype(BF16)


def layer(start, up_ids, down_ids, live, acts, carried, weights):
    slots = HALF // CHUNKS
    first = not carried
    smem = pl.BlockSpec(memory_space=pltpu.SMEM)
    anys = pl.BlockSpec(memory_space=pl.ANY)
    whole = pl.BlockSpec((32, 2, BLK, BLK), lambda s: (0, 0, 0, 0), pipeline_mode=pl.Buffered(1))
    near = [pl.BlockSpec((w.shape[0], 1, 3, BLK, BLK), lambda s: (0, start + s, 0, 0, 0)) for w in weights[:5]]
    far = [pl.BlockSpec((w.shape[0], 1, 3, BLK, BLK), lambda s: (0, s, 0, 0, 0)) for w in weights[5:]]
    part = jax.ShapeDtypeStruct((32, 2, BLK, BLK), BF16)
    outs = pl.pallas_call(
        functools.partial(layer_kernel, first, slots),
        grid=(slots,),
        in_specs=[smem] * 3 + [anys] * 2 + [whole] * len(carried[:2]) + [anys] * len(carried[2:]) + near + far,
        out_specs=[whole] * 2 + near + far,
        out_shape=[part] * 2 + [jax.ShapeDtypeStruct(w.shape, BF16) for w in weights],
        input_output_aliases={} if first else {7 + i: 2 + i for i in range(5)},
        scratch_shapes=[
            pltpu.VMEM((2, 32, 2, BLK, BLK), BF16),
            pltpu.VMEM((32, 2, 2 * BLK, BLK), F32),
            pltpu.VMEM((2 * BLK, 2048), BF16),
            pltpu.VMEM((2 * BLK, 2048), BF16),
            pltpu.VMEM((2048, 2 * BLK), BF16),
            pltpu.VMEM((BLK, 2048), BF16),
            pltpu.SemaphoreType.DMA((2,)),
        ],
        compiler_params=pltpu.CompilerParams(vmem_limit_bytes=60 * 1024 * 1024),
        cost_estimate=pl.CostEstimate(
            flops=LONG, bytes_accessed=16 * 1024 * 1024, transcendentals=0
        ),
        name="layer",
    )(up_ids, down_ids, live, *acts, *carried, *weights)
    return outs[:2], outs[2:7], outs[7:]


def tables(owner, up_rows, down_cols):
    zh, x, c = (lax.axis_index(a) for a in ("zh", "x", "c"))
    zl = lax.axis_index("zl")
    me = lax.axis_index("y") * 4 + zl
    count = owner.shape[0]
    f = jnp.arange(count, dtype=jnp.int32)
    earlier = (owner[None, :] == me) & (f[None, :] < f[:, None])
    rank = jnp.sum(earlier.astype(jnp.int32), 1)
    slot = c * HALF + jnp.arange(HALF, dtype=jnp.int32)
    select = ((owner == me)[None, :] & (rank[None, :] == slot[:, None])).astype(jnp.int32)
    away = jnp.array([0, 0, 1, 1, 3, 3, 2, 2] * 2, jnp.int32)
    b = jnp.arange(16, dtype=jnp.int32)
    held = (zh ^ (b // 8)) * 8 + ((x - away) % 4) * 2 + (c ^ (b % 2))

    def ids(table):
        raw = jnp.sum(select[:, :, None] * jnp.take(table, held, axis=1)[None], 1)
        home = raw // 2
        return ((home // 4) * 4 + (zl - home % 4) % 4) * 2 + raw % 2

    live = jnp.sum(select, 1).astype(F32)
    return ids(up_rows), ids(down_cols), live


def add(*values):
    return sum(v.astype(F32) for v in values)


tie = lax.optimization_barrier


def neighbours(value):
    return rot(value, "x", 1), rot(value, "x", -1)


def copy_kernel(*refs):
    for source, target in zip(refs[: len(refs) // 2], refs[len(refs) // 2 :]):
        target[...] = source[...]


def add_kernel(left, right, from_right, from_left, new_left, new_right):
    new_left[0] = (left[0].astype(F32) + from_right[0].astype(F32)).astype(BF16)
    new_left[1] = left[1]
    new_right[0] = right[0]
    new_right[1] = (right[1].astype(F32) + from_left[0].astype(F32)).astype(BF16)


def small(kernel, values, shapes, earlier=(), flops=SHORT):
    whole = [pl.BlockSpec(memory_space=pltpu.VMEM)] * len(shapes)
    count = len(values)

    def body(*refs):
        kernel(*refs[:count], *refs[count + len(earlier) :])

    return pl.pallas_call(
        body,
        in_specs=[pl.BlockSpec(memory_space=pltpu.VMEM)] * count + [pl.BlockSpec(memory_space=pl.ANY)] * len(earlier),
        out_specs=whole,
        out_shape=[jax.ShapeDtypeStruct(v, BF16) for v in shapes],
        compiler_params=pltpu.CompilerParams(vmem_limit_bytes=32 * 1024 * 1024),
        cost_estimate=pl.CostEstimate(flops=flops, bytes_accessed=2 * 1024 * 1024, transcendentals=0),
        name=kernel.__name__,
    )(*values, *earlier)


def halves_kernel(left, right, first, second):
    first[...] = left[0:1]
    second[...] = right[1:2]


def shards(tokens, cotangent, gate_blocks, up_blocks, down_blocks, owner, up_rows, down_cols):
    c = lax.axis_index("c")
    up_ids, down_ids, live = tables(owner, up_rows, down_cols)

    blocks = (gate_blocks, up_blocks, down_blocks)
    mine = jnp.stack([lax.dynamic_slice_in_dim(v, c * HALF, HALF, 0) for v in blocks], 1)
    theirs = jnp.stack([lax.dynamic_slice_in_dim(v, (1 - c) * HALF, HALF, 0) for v in blocks], 1)
    base = jnp.stack([mine, rot(theirs, "c", 1)])

    acts = jnp.stack([tokens, cotangent]).reshape(2, BLK, 2, BLK).transpose(2, 0, 1, 3)
    base, acts, up_ids, down_ids, live = tie((base, acts, up_ids, down_ids, live))
    lines = [small(copy_kernel, (acts,), [acts.shape])[0]] + [rot(acts, "zl", k) for k in (1, 2, 3)]
    near = neighbours(base)
    line, base = tie((jnp.concatenate(lines), base))
    ring = lax.all_gather(line, "y", axis=0, tiled=True)

    size = HALF // CHUNKS
    takes = [slice(n * size, (n + 1) * size) for n in range(CHUNKS)]
    first, second = [rot(base[:, take], "zh", 1) for take in takes]
    cut = small(halves_kernel, near, [(1, *base.shape[1:])] * 2)
    near = [base, *near, rot(cut[0], "x", 1), rot(cut[1], "x", -1)]
    first, near = tie((first, near))
    first = [first, *[rot(first, "x", k) for k in (1, 3, 2)]]
    second, first, ring = tie((second, first, ring))
    second = [second, *[rot(second, "x", k) for k in (1, 3, 2)]]
    ring = [ring, rot(ring, "c", 1)]

    take = takes[0]
    parts, near_parts, far_parts = layer(0, up_ids[take], down_ids[take], live[take], ring, (), near + first)
    first_sum = add(far_parts[0], *[rot(far_parts[p], "x", k) for p, k in ((1, 3), (2, 1), (3, 2))]).astype(BF16)
    take = takes[1]
    parts, near_parts, far_parts = layer(
        size, up_ids[take], down_ids[take], live[take], ring, (*parts, *near_parts), near + second
    )
    parts, far_parts, near_parts, first_sum = tie((parts, far_parts, near_parts, first_sum))
    both = add(parts[0], rot(parts[1], "c", 1)).astype(BF16)
    first_sum = rot(first_sum, "zh", 1)
    second_sum = [far_parts[0], *[rot(far_parts[p], "x", k) for p, k in ((1, 3), (2, 1), (3, 2))]]
    line = lax.psum_scatter(both, "y", scatter_dimension=0, tiled=True)
    sent = small(copy_kernel, near_parts[3:], [v.shape for v in near_parts[3:]], [both], LONG)
    second_sum, sent, first_sum = tie((second_sum, sent, first_sum))
    second_sum = add(*second_sum).astype(BF16)
    crossed = rot(sent[0], "x", -1), rot(sent[1], "x", 1)
    left, right = small(add_kernel, (*near_parts[1:3], *crossed), [near_parts[1].shape] * 2, [second_sum])
    second_sum = rot(second_sum, "zh", 1)
    near_sum = add(near_parts[0], rot(left, "x", -1), rot(right, "x", 1))
    line = line.reshape(4, 2, 2, BLK, BLK)
    lines = [line[0], *[rot(line[k], "zl", -k) for k in (1, 2, 3)]]
    near_sum, lines, second_sum = tie((near_sum, lines, second_sum))
    done = add(*lines).astype(BF16)
    done = done.transpose(1, 2, 0, 3).reshape(2, BLK, 2 * BLK)
    far_sums = [first_sum, second_sum]

    total = add(near_sum, jnp.concatenate(far_sums, 1))
    received = rot(total[1].astype(BF16), "c", 1).astype(F32)
    lower = jnp.where(c == 0, total[0], received)
    upper = jnp.where(c == 0, received, total[0])
    grads = [jnp.concatenate([lower[:, i], upper[:, i]]) for i in range(3)]
    return (done[0], done[1], *grads)


def solution(mesh):
    fine = Mesh(mesh.devices.reshape(2, 4, 2, 4, 4), ("zh", "x", "c", "y", "zl"))
    dp = ("zh", "x", "c")
    mp = ("y", "zl")
    return jax.shard_map(
        shards,
        mesh=fine,
        in_specs=(P(dp, mp), P(dp, mp), P(mp, dp, None), P(mp, dp, None), P(mp, None, dp), P(), P(), P()),
        out_specs=(P(dp, mp), P(dp, mp), P(mp, dp, None), P(mp, dp, None), P(mp, None, dp)),
        check_vma=False,
    )
```
